768 devices in a mesh: grp: 8 (over y), own: 8 (over x, core), rep: 12 (over z).
Axes of the slice: x: 4, y: 8, z: 12, core: 2. Of those that a mesh axis runs over, the one named last changes fastest.
Arguments:
- self_feat: bfloat16 [786432, 256], P(('grp', 'own', 'rep')), may hold values from -6 to 6
- neighbor: int32 [786432, 15], P(('grp', 'own', 'rep')), may hold values from 0 to 2815
- grad_out: bfloat16 [786432, 256], P(('grp', 'own', 'rep')), may hold values from -0.015625 to 0.015625
- fetch_rows: int32 [6144, 96], P(('grp', 'own', 'rep')), may hold values from 0 to 4095
- fetch_count: int32 [6144], P(('grp', 'own', 'rep')), may hold values from 12 to 96, as said below
- table_codes: bfloat16 [32768, 256], P('own'), may hold values from -6 to 6
- table_scale: bfloat16 [32768, 2], P('own'), may hold values from 0.5 to 2
- hot_table: bfloat16 [2048, 256], replicated, may hold values from -6 to 6
- self_weight: bfloat16 [256, 256], replicated, may hold values from -0.375 to 0.375
- neighbor_weight: bfloat16 [256, 256], replicated, may hold values from -0.375 to 0.375
Outputs:
- hidden: bfloat16 [786432, 256], P(('grp', 'own', 'rep'))
- self_grad: float32 [256, 256], replicated
- neighbor_grad: float32 [256, 256], replicated
The draws below stay inside these ranges and needn't reach their ends.
Inputs may be any that keep to these rules, and one draw needn't show every extreme that they name: `fetch_count`: in every group of devices sharing grp and rep indices, one owner is asked for exactly 96 rows by every device of the group; other counts lie from 12 to 48.
All inputs are finite; a program needn't handle non-finite values.
Results may differ from the reference program's by a relative error of at most 0.0056.
Values may be sent and summed in bfloat16 or wider, within the bound.
No kernel may reach another device: no remote copies, remote signals or barrier semaphores. Data moves between devices by JAX's collectives and lax.ppermute only.
A program may use at most 128 MiB of HBM per device.

```python
import math
import jax
import jax.numpy as jnp
from jax import lax

F = 256
H = 256
SB = 128
K = 15
B = 1024
CAP = 96
HOT = 2048
ROWS_OWN = 4096
NB = 2
TARGETS = 786432
ROWS = 32768
POOL = 2816
N_GRP = 8
N_OWN = 8
N_REP = 12
DEVICES = 768


def draw_fetch_count(key, part):
    key = jax.random.fold_in(key, 7)
    first, second = jax.random.split(key)
    heavy = jax.random.randint(first, (N_GRP, 1, N_REP, 1), 0, N_OWN)
    lower = jax.random.randint(second, (N_GRP, N_OWN, N_REP, N_OWN), CAP // 8, CAP // 2 + 1)
    owners = jnp.arange(N_OWN, dtype=jnp.int32).reshape(1, 1, 1, N_OWN)
    counts = jnp.where(owners == heavy, CAP, lower)
    return counts.reshape(-1).astype(jnp.int32)


def set_ends(result, rng, low, high):
    shape = result.shape
    index_at = [jax.random.randint(jax.random.fold_in(rng, axis), (), 0, shape[axis]) for axis in range(len(shape))]
    result = result.at[tuple(index_at)].set(low)
    longest = shape.index(max(shape))
    index_at[longest] = (index_at[longest] + 1) % shape[longest]
    return result.at[tuple(index_at)].set(high)


def shard_levels(stream_key, dims, shards, low, largest):
    def one(axis_at, blocks):
        draws = jax.random.uniform(jax.random.fold_in(jax.random.fold_in(stream_key, 6), axis_at), (blocks,), jnp.float32, low / len(shards), largest / len(shards))
        return jnp.repeat(jnp.exp(draws), dims[axis_at] // blocks).reshape((-1,) + (1,) * (len(dims) - axis_at - 1))

    level = one(*shards[0])
    for cut in shards[1:]:
        level = level * one(*cut)
    return level


def bell_draw(own_key, shape, deviation, bound, cuts=(), held_as=jnp.bfloat16):
    loudness = shard_levels(own_key, shape, cuts, -0.22, 0.18) if cuts else 1.0
    array = jax.random.normal(own_key, shape, jnp.float32) * deviation * loudness
    return jnp.minimum(jnp.maximum(array, -bound), bound).astype(held_as)


def setup_inputs(seed: int = 0) -> dict:
    arg_keys = jax.random.split(jax.random.key(seed), 11)
    return {
        "self_feat": bell_draw(arg_keys[0], (TARGETS, F), 1.0, 6.0, ((0, 768),)),
        "neighbor": set_ends(jax.random.randint(arg_keys[1], (TARGETS, K), 0, POOL), jax.random.fold_in(arg_keys[1], 1), 0, POOL - 1).astype(jnp.int32),
        "grad_out": bell_draw(arg_keys[2], (TARGETS, H), (TARGETS ** -0.5), 0.015625, ((0, 768),)),
        "fetch_rows": set_ends(jax.random.randint(arg_keys[3], (DEVICES * N_OWN, CAP), 0, ROWS_OWN), jax.random.fold_in(arg_keys[3], 1), 0, ROWS_OWN - 1).astype(jnp.int32),
        "fetch_count": draw_fetch_count(jax.random.fold_in(arg_keys[10], 71), 0),
        "table_codes": bell_draw(arg_keys[5], (ROWS, F), 1.0, 6.0, ((0, 8),)),
        "table_scale": jnp.clip(jnp.exp(math.log(2.0) - 1.3862944 * jax.random.uniform(arg_keys[6], (ROWS, NB), jnp.float32) ** shard_levels(arg_keys[6], (ROWS, NB), ((0, 8),), -0.2, 0.2)), 0.5, 2.0).astype(jnp.bfloat16),
        "hot_table": bell_draw(arg_keys[7], (HOT, F), 1.0, 6.0),
        "self_weight": bell_draw(arg_keys[8], (F, H), F ** -0.5, 0.375),
        "neighbor_weight": bell_draw(arg_keys[9], (F, H), F ** -0.5, 0.375),
    }


def silu_slope(value):
    sigma = jax.nn.sigmoid(value)
    return sigma * (1.0 + value * (1.0 - sigma))


def reference(self_feat, neighbor, grad_out, fetch_rows, fetch_count, table_codes, table_scale, hot_table, self_weight, neighbor_weight):
    ndev = N_GRP * N_OWN * N_REP
    feat_dev = self_feat.reshape(ndev, B, F)
    nbr_dev = neighbor.reshape(ndev, B, K)
    grad_dev = grad_out.reshape(ndev, B, H)
    rows_dev = fetch_rows.reshape(ndev, N_OWN, CAP)
    count_dev = fetch_count.reshape(ndev, N_OWN)
    row_base = (jnp.arange(N_OWN, dtype=jnp.int32) * ROWS_OWN)[:, None]
    slot_index = jnp.arange(CAP, dtype=jnp.int32)[None, :]

    def one_device(carry, inputs):
        own_feat, own_nbr, own_grad, own_rows, own_count = inputs
        indices = (own_rows + row_base).reshape(-1)
        code_rows = table_codes[indices].astype(jnp.float32).reshape(N_OWN * CAP, NB, SB)
        scales = table_scale[indices].astype(jnp.float32)[:, :, None]
        slot_live = (slot_index < own_count[:, None]).reshape(-1)
        decoded = (code_rows * scales).reshape(N_OWN * CAP, F)
        cold_rows = jnp.where(slot_live[:, None], decoded, jnp.zeros_like(decoded)).astype(jnp.bfloat16)
        pool_rows = jnp.concatenate([hot_table, cold_rows], axis=0)
        pool_live = jnp.concatenate([jnp.ones((HOT,), jnp.int32), slot_live.astype(jnp.int32)])
        picked = pool_rows[own_nbr]
        summed = own_feat.astype(jnp.float32) + jnp.sum(picked.astype(jnp.float32), axis=1)
        divisor = (1 + jnp.sum(pool_live[own_nbr], axis=1)).astype(jnp.float32)
        mean_feat = (summed / divisor[:, None]).astype(jnp.bfloat16)
        preact = jnp.dot(own_feat, self_weight, preferred_element_type=jnp.float32) + jnp.dot(mean_feat, neighbor_weight, preferred_element_type=jnp.float32)
        hidden = jax.nn.silu(preact).astype(jnp.bfloat16)
        delta = (own_grad.astype(jnp.float32) * silu_slope(preact)).astype(jnp.bfloat16)
        grad_self = carry[0] + jnp.dot(own_feat.T, delta, preferred_element_type=jnp.float32)
        grad_nbr = carry[1] + jnp.dot(mean_feat.T, delta, preferred_element_type=jnp.float32)
        return (grad_self, grad_nbr), hidden

    zeros = jnp.zeros((F, H), jnp.float32)
    (grad_self, grad_nbr), hidden = lax.scan(one_device, (zeros, zeros), (feat_dev, nbr_dev, grad_dev, rows_dev, count_dev))
    return hidden.reshape(TARGETS, H), grad_self, grad_nbr
```

```python
import jax
import jax.numpy as jnp
from jax import lax
from jax.experimental import pallas as pl
from jax.experimental.pallas import tpu as pltpu
from jax.sharding import PartitionSpec as P

F32 = jnp.float32
BF16 = jnp.bfloat16
LANES = 128
STEP = 16


def count_kernel(nbr_ref, self_ref, hot_ref, sum_ref, cold_ref, cols_ref, counts_ref):
    neighbors, targets = nbr_ref.shape
    hot_blocks = hot_ref.shape[0] // LANES
    cold_blocks = cold_ref.shape[1] // LANES
    blocks = hot_blocks + cold_blocks
    groups = (blocks + 7) // 8
    rows = nbr_ref[...]
    pad = jnp.zeros((16 - neighbors, targets), jnp.int32)
    cols_ref[...] = jnp.concatenate([rows, pad], axis=0).T
    lane = lax.broadcasted_iota(jnp.int32, (STEP, LANES), 1)

    def step(i, carry):
        at = pl.ds(pl.multiple_of(i * STEP, STEP), STEP)
        own = cols_ref[at, :]
        words = [jnp.zeros((STEP, LANES), jnp.int32) for _ in range(groups)]
        for k in range(neighbors):
            row = jnp.broadcast_to(own[:, k : k + 1], (STEP, LANES))
            bit = jnp.left_shift(jnp.int32(1), jnp.bitwise_and(jnp.right_shift(row, 5), 28))
            key = jnp.bitwise_and(row, ~0x380)
            for g in range(groups):
                words[g] = words[g] + jnp.where(key == lane + g * 1024, bit, 0)
        for b in range(blocks):
            word = words[b // 8]
            if b % 8:
                word = lax.shift_right_logical(word, 4 * (b % 8))
            count = jnp.bitwise_and(word, 15).astype(F32).astype(BF16)
            if b < hot_blocks:
                counts_ref[at, b * LANES : (b + 1) * LANES] = count
            else:
                c = b - hot_blocks
                cold_ref[at, c * LANES : (c + 1) * LANES] = count
        return carry

    lax.fori_loop(0, targets // STEP, step, 0, unroll=2)
    sum_ref[...] = self_ref[...].astype(F32) + jnp.dot(
        counts_ref[...], hot_ref[...], preferred_element_type=F32
    )


def decode_kernel(code_ref, scale_ref, out_ref):
    blocks = scale_ref.shape[0]
    width = code_ref.shape[1]
    which = lax.broadcasted_iota(jnp.int32, (blocks, width), 0)
    block = lax.broadcasted_iota(jnp.int32, (blocks, width), 1) // (width // blocks)
    ones = jnp.where(which == block, 1.0, 0.0).astype(BF16)
    scale = lax.dot_general(
        scale_ref[...], ones, (((0,), (0,)), ((), ())), preferred_element_type=F32
    )
    out_ref[...] = (code_ref[...].astype(F32) * scale).astype(BF16)


def select_kernel(want_ref, table_ref, out_ref, cols_ref):
    peers, slots = want_ref.shape
    rows = table_ref.shape[0]
    cols_ref[...] = want_ref[...].T
    lane = lax.broadcasted_iota(jnp.int32, (slots, rows), 1)
    for p in range(peers):
        want = jnp.broadcast_to(cols_ref[:, p : p + 1], (slots, rows))
        pick = jnp.where(want == lane, 1.0, 0.0).astype(BF16)
        out_ref[p] = jnp.dot(pick, table_ref[...], preferred_element_type=F32).astype(BF16)


def layer_kernel(
    live_ref,
    sum_ref,
    counts_ref,
    rows_ref,
    self_ref,
    grad_ref,
    self_w_ref,
    nbr_w_ref,
    hidden_ref,
    grads_ref,
    cold_ref,
    dead_ref,
    total_ref,
):
    owners, slots, width = rows_ref.shape
    step = pl.program_id(0)

    @pl.when(step == 0)
    def _():
        for p in range(owners):
            at = slice(p * slots, (p + 1) * slots)
            slot = lax.broadcasted_iota(jnp.int32, (slots, width), 0)
            live = slot < live_ref[p]
            cold_ref[at, :] = jnp.where(live, rows_ref[p].astype(F32), 0.0).astype(BF16)
            dead_ref[at, :] = jnp.where(live[:, :LANES], 0.0, 1.0).astype(BF16)
        total_ref[...] = jnp.zeros_like(total_ref)

    counts = counts_ref[...]
    summed = sum_ref[...] + jnp.dot(counts, cold_ref[...], preferred_element_type=F32)
    dead = jnp.dot(counts, dead_ref[...], preferred_element_type=F32)
    share = 1.0 / (16.0 - dead)
    share = jnp.concatenate([share] * (width // LANES), axis=1)
    mean = (summed * share).astype(BF16)
    own = self_ref[...]
    pre = jnp.dot(own, self_w_ref[...], preferred_element_type=F32) + jnp.dot(
        mean, nbr_w_ref[...], preferred_element_type=F32
    )
    sigma = 1.0 / (1.0 + jnp.exp(-pre))
    hidden_ref[...] = (pre * sigma).astype(BF16)
    slope = sigma * (1.0 + pre * (1.0 - sigma))
    delta = (grad_ref[...].astype(F32) * slope).astype(BF16)
    across = (((0,), (0,)), ((), ()))
    total_ref[:width, :] += lax.dot_general(own, delta, across, preferred_element_type=F32)
    total_ref[width:, :] += lax.dot_general(mean, delta, across, preferred_element_type=F32)

    @pl.when(step == pl.num_programs(0) - 1)
    def _():
        grads_ref[...] = total_ref[...].astype(BF16)


def whole(shape):
    return pl.BlockSpec(shape, lambda i: (0,) * len(shape))


def count_rows(neighbor, self_feat, hot_table, cold):
    targets, width = self_feat.shape
    neighbors = neighbor.shape[1]
    hot = hot_table.shape[0]
    tile = 256
    return pl.pallas_call(
        count_kernel,
        grid=(targets // tile,),
        in_specs=[
            pl.BlockSpec((neighbors, tile), lambda i: (0, i)),
            pl.BlockSpec((tile, width), lambda i: (i, 0)),
            whole((hot, width)),
        ],
        out_specs=[
            pl.BlockSpec((tile, width), lambda i: (i, 0)),
            pl.BlockSpec((tile, cold), lambda i: (i, 0)),
        ],
        out_shape=[
            jax.ShapeDtypeStruct((targets, width), F32),
            jax.ShapeDtypeStruct((targets, cold), BF16),
        ],
        scratch_shapes=[pltpu.VMEM((tile, 16), jnp.int32), pltpu.VMEM((tile, hot), BF16)],
        cost_estimate=pl.CostEstimate(
            flops=2 * targets * hot * width, bytes_accessed=16 * 2**20, transcendentals=0
        ),
        compiler_params=pltpu.CompilerParams(vmem_limit_bytes=32 * 2**20),
        name="count_rows",
    )(neighbor.T, self_feat, hot_table)


def decode_table(codes, scale):
    rows, width = codes.shape
    blocks = scale.shape[1]
    tile = 1024
    return pl.pallas_call(
        decode_kernel,
        grid=(rows // tile,),
        in_specs=[
            pl.BlockSpec((tile, width), lambda i: (i, 0)),
            pl.BlockSpec((blocks, tile), lambda i: (0, i)),
        ],
        out_specs=pl.BlockSpec((tile, width), lambda i: (i, 0)),
        out_shape=jax.ShapeDtypeStruct((rows, width), BF16),
        cost_estimate=pl.CostEstimate(
            flops=2 * rows * width, bytes_accessed=4 * 2**20, transcendentals=0
        ),
        compiler_params=pltpu.CompilerParams(vmem_limit_bytes=32 * 2**20),
        name="decode_table",
    )(codes, scale.T)


def select_rows(wanted, table):
    peers, slots = wanted.shape
    rows, width = table.shape
    return pl.pallas_call(
        select_kernel,
        out_shape=jax.ShapeDtypeStruct((peers, slots, width), BF16),
        scratch_shapes=[pltpu.VMEM((slots, peers), jnp.int32)],
        cost_estimate=pl.CostEstimate(
            flops=2 * peers * slots * rows * width, bytes_accessed=3 * 2**20, transcendentals=0
        ),
        compiler_params=pltpu.CompilerParams(vmem_limit_bytes=32 * 2**20),
        name="select_rows",
    )(wanted, table)


def layer(live, summed, counts, rows, self_feat, grad_out, self_weight, neighbor_weight):
    targets, width = self_feat.shape
    cold = counts.shape[1]
    tile = 256
    by_tile = lambda w: pl.BlockSpec((tile, w), lambda i: (i, 0))
    return pl.pallas_call(
        layer_kernel,
        grid=(targets // tile,),
        in_specs=[
            pl.BlockSpec(memory_space=pltpu.SMEM),
            by_tile(width),
            by_tile(cold),
            whole(rows.shape),
            by_tile(width),
            by_tile(width),
            whole(self_weight.shape),
            whole(neighbor_weight.shape),
        ],
        out_specs=[by_tile(width), whole((2 * width, width))],
        out_shape=[
            jax.ShapeDtypeStruct((targets, width), BF16),
            jax.ShapeDtypeStruct((2 * width, width), BF16),
        ],
        scratch_shapes=[
            pltpu.VMEM((cold, width), BF16),
            pltpu.VMEM((cold, LANES), BF16),
            pltpu.VMEM((2 * width, width), F32),
        ],
        cost_estimate=pl.CostEstimate(
            flops=2 * targets * width * (cold + 4 * width),
            bytes_accessed=5 * 2**20,
            transcendentals=targets * width,
        ),
        compiler_params=pltpu.CompilerParams(vmem_limit_bytes=32 * 2**20),
        name="layer",
    )(live, summed, counts, rows, self_feat, grad_out, self_weight, neighbor_weight)


def exchange(parts, axes):
    return lax.all_to_all(parts, axes, split_axis=0, concat_axis=0, tiled=True)


def sum_everywhere(grads):
    rows, width = grads.shape
    plane = ("grp", "own")
    peers = lax.axis_size("grp") * lax.axis_size("own")
    depth = lax.axis_size("rep")
    parts = exchange(grads.reshape(peers, rows // peers, width), plane)
    share = jnp.sum(parts.astype(F32), axis=0)
    shares = exchange(jnp.broadcast_to(share[None], (depth,) + share.shape), "rep")
    share = jnp.sum(shares, axis=0).astype(BF16)
    parts = exchange(jnp.broadcast_to(share[None], (peers,) + share.shape), plane)
    return parts.reshape(rows, width).astype(F32)


def body(
    self_feat,
    neighbor,
    grad_out,
    fetch_rows,
    fetch_count,
    table_codes,
    table_scale,
    hot_table,
    self_weight,
    neighbor_weight,
):
    owners, slots = fetch_rows.shape
    width = self_feat.shape[1]
    wanted = exchange(fetch_rows, "own")
    table = decode_table(table_codes, table_scale)
    summed, counts = count_rows(neighbor, self_feat, hot_table, owners * slots)
    rows = exchange(select_rows(wanted, table), "own")
    hidden, grads = layer(
        fetch_count, summed, counts, rows, self_feat, grad_out, self_weight, neighbor_weight
    )
    total = sum_everywhere(grads)
    return hidden, total[:width], total[width:]


def solution(mesh):
    split = P(("grp", "own", "rep"), None)
    in_specs = (
        split,
        split,
        split,
        split,
        P(("grp", "own", "rep")),
        P("own", None),
        P("own", None),
        P(),
        P(),
        P(),
    )
    out_specs = (split, P(), P())
    return jax.shard_map(body, mesh=mesh, in_specs=in_specs, out_specs=out_specs, check_vma=False)
```

```python
import jax
import jax.numpy as jnp
from jax import lax
from jax.experimental import pallas as pl
from jax.experimental.pallas import tpu as pltpu
from jax.sharding import PartitionSpec as P

F32 = jnp.float32
BF16 = jnp.bfloat16
LANES = 128
STEP = 16
PEERS = 4
PARTS = 4
VMEM = 32 * 2**20


def counter(words, i):
    if i:
        words = lax.shift_right_logical(words, 4 * i)
    if i < 7:
        words = jnp.bitwise_and(words, 15)
    return words.astype(F32).astype(BF16)


def count_kernel(
    nbr_hbm,
    hot_hbm,
    self_hbm,
    grad_hbm,
    self_w_hbm,
    nbr_w_hbm,
    sum_ref,
    cold_ref,
    held_ref,
    nbr_ref,
    hot_ref,
    keys_ref,
    counts_ref,
    sems,
):
    moves = [(nbr_hbm, nbr_ref), (hot_hbm, hot_ref)]
    start = 0
    for array in (self_hbm, grad_hbm, self_w_hbm, nbr_w_hbm):
        moves.append((array, held_ref.at[start : start + array.shape[0]]))
        start += array.shape[0]
    copies = [pltpu.make_async_copy(*move, sems.at[i]) for i, move in enumerate(moves)]
    for copy in copies:
        copy.start()
    neighbors, targets = nbr_ref.shape
    hot_blocks = hot_ref.shape[0] // LANES
    groups = hot_blocks // 8 + 1
    steps = LANES // STEP

    copies[0].wait()
    rows = nbr_ref[...]
    keys_ref[0, :neighbors, :] = jnp.bitwise_and(rows, LANES - 1)
    bit = jnp.left_shift(jnp.int32(1), jnp.bitwise_and(jnp.right_shift(rows, 5), 28))
    group = jnp.right_shift(rows, 10)
    for g in range(groups):
        keys_ref[1 + g, :neighbors, :] = jnp.where(group == g, bit, 0)

    def step(i, carry):
        cut = pl.ds(pl.multiple_of((i // steps) * LANES, LANES), LANES)
        base = pl.multiple_of((i % steps) * STEP, STEP)
        place = lax.broadcasted_iota(jnp.int32, (STEP, LANES), 0) + base
        words = [jnp.zeros((STEP, LANES), jnp.int32) for _ in range(groups)]
        for k in range(neighbors):
            spread = lambda r: jnp.broadcast_to(keys_ref[r, k : k + 1, cut], (STEP, LANES))
            here = spread(0) == place
            for g in range(groups):
                words[g] = words[g] + jnp.where(here, spread(1 + g), 0)
        for b in range(hot_blocks):
            counts_ref[pl.ds(b * LANES + base, STEP), cut] = counter(words[b // 8], b % 8)
        cold_ref[pl.ds(base, STEP), cut] = words[groups - 1]
        return carry

    lax.fori_loop(0, (targets // LANES) * steps, step, 0, unroll=2)
    for copy in copies[1:]:
        copy.wait()
    sum_ref[...] = held_ref[:targets, :].astype(F32).T + lax.dot_general(
        hot_ref[...], counts_ref[...], (((0,), (0,)), ((), ())), preferred_element_type=F32
    )


def decode_kernel(code_hbm, scale_hbm, out_ref, code_ref, scale_ref, sems):
    rows, width = code_ref.shape
    blocks = scale_ref.shape[0]
    part = rows // PARTS
    scale_copy = pltpu.make_async_copy(scale_hbm, scale_ref, sems.at[PARTS])
    scale_copy.start()
    cuts = [slice(i * part, (i + 1) * part) for i in range(PARTS)]
    copies = [
        pltpu.make_async_copy(code_hbm.at[cut], code_ref.at[cut], sems.at[i])
        for i, cut in enumerate(cuts)
    ]
    for copy in copies:
        copy.start()
    which = lax.broadcasted_iota(jnp.int32, (blocks, width), 0)
    block = lax.broadcasted_iota(jnp.int32, (blocks, width), 1) // (width // blocks)
    ones = jnp.where(which == block, 1.0, 0.0).astype(BF16)
    scale_copy.wait()
    for cut, copy in zip(cuts, copies):
        scale = lax.dot_general(
            scale_ref[:, cut], ones, (((0,), (0,)), ((), ())), preferred_element_type=F32
        )
        copy.wait()
        out_ref[cut] = (code_ref[cut].astype(F32) * scale).astype(BF16)


def select_kernel(want_ref, table_ref, out_ref, cols_ref):
    peers, slots = want_ref.shape
    rows, width = table_ref.shape
    cols_ref[...] = want_ref[...].T
    lane = lax.broadcasted_iota(jnp.int32, (slots, rows), 1)
    for p in range(0, peers, PEERS):
        picks = [
            jnp.where(jnp.broadcast_to(cols_ref[:, q : q + 1], (slots, rows)) == lane, 1.0, 0.0)
            for q in range(p, p + PEERS)
        ]
        pick = jnp.concatenate(picks, axis=0).astype(BF16)
        found = jnp.dot(pick, table_ref[...], preferred_element_type=F32).astype(BF16)
        out_ref[p : p + PEERS] = found.reshape(PEERS, slots, width)


def layer_kernel(
    live_ref,
    sum_ref,
    words_ref,
    rows_ref,
    held_ref,
    hidden_hbm,
    grads_ref,
    cold_ref,
    hidden_ref,
    sem,
):
    owners, slots, width = rows_ref.shape
    targets = sum_ref.shape[1]
    rows = []
    for p in range(owners):
        slot = lax.broadcasted_iota(jnp.int32, (slots, width), 0)
        rows.append(jnp.where(slot < live_ref[p], rows_ref[p].astype(F32), 0.0))
    cold_ref[:width, :] = jnp.concatenate(rows, axis=0).T.astype(BF16)
    dead = [
        jnp.where(lax.broadcasted_iota(jnp.int32, (1, slots), 1) < live_ref[p], 0.0, 1.0)
        for p in range(owners)
    ]
    dead = jnp.broadcast_to(jnp.concatenate(dead, axis=1), (STEP, owners * slots))
    cold_ref[width:, :] = dead.astype(BF16)

    words = words_ref[...]
    blocks = owners * slots // LANES
    counts = jnp.concatenate([counter(words, b) for b in range(blocks)], axis=0)
    cold = jnp.dot(cold_ref[...], counts, preferred_element_type=F32)
    share = 1.0 / (16.0 - cold[width : width + 1, :])
    mean_t = ((sum_ref[...] + cold[:width, :]) * share).astype(BF16)
    mean = mean_t.T
    own = held_ref[:targets, :]
    weights = 2 * targets
    pre = jnp.dot(own, held_ref[weights : weights + width, :], preferred_element_type=F32) + jnp.dot(
        mean, held_ref[weights + width :, :], preferred_element_type=F32
    )
    sigma = 1.0 / (1.0 + jnp.exp(-pre))
    hidden_ref[...] = (pre * sigma).astype(BF16)
    out = pltpu.make_async_copy(hidden_ref, hidden_hbm, sem)
    out.start()
    slope = sigma * (1.0 + pre * (1.0 - sigma))
    delta = (held_ref[targets:weights, :].astype(F32) * slope).astype(BF16)
    across = (((0,), (0,)), ((), ()))
    grads_ref[:width, :] = lax.dot_general(
        own, delta, across, preferred_element_type=F32
    ).astype(BF16)
    grads_ref[width:, :] = jnp.dot(mean_t, delta, preferred_element_type=F32).astype(BF16)
    out.wait()


def outside(array):
    return pltpu.with_memory_space_constraint(array, pltpu.HBM)


def inside(array):
    return pltpu.with_memory_space_constraint(array, pltpu.VMEM)


def count_rows(neighbor, hot_table, self_feat, grad_out, self_weight, neighbor_weight):
    targets, width = self_feat.shape
    neighbors = neighbor.shape[1]
    hot = hot_table.shape[0]
    passed = (self_feat, grad_out, self_weight, neighbor_weight)
    arrays = (neighbor.T, hot_table) + passed
    return pl.pallas_call(
        count_kernel,
        in_specs=[pl.BlockSpec(memory_space=pltpu.HBM)] * len(arrays),
        out_shape=[
            jax.ShapeDtypeStruct((width, targets), F32),
            jax.ShapeDtypeStruct((LANES, targets), jnp.int32),
            jax.ShapeDtypeStruct((sum(array.shape[0] for array in passed), width), BF16),
        ],
        scratch_shapes=[
            pltpu.VMEM((neighbors, targets), jnp.int32),
            pltpu.VMEM((hot, width), BF16),
            pltpu.VMEM((4, 16, targets), jnp.int32),
            pltpu.VMEM((hot, targets), BF16),
            pltpu.SemaphoreType.DMA((len(arrays),)),
        ],
        cost_estimate=pl.CostEstimate(
            flops=2 * targets * hot * width, bytes_accessed=16 * 2**20, transcendentals=0
        ),
        compiler_params=pltpu.CompilerParams(vmem_limit_bytes=VMEM),
        name="count_rows",
    )(*map(outside, arrays))


def decode_table(codes, scale):
    rows, width = codes.shape
    blocks = scale.shape[1]
    return pl.pallas_call(
        decode_kernel,
        in_specs=[pl.BlockSpec(memory_space=pltpu.HBM)] * 2,
        out_shape=jax.ShapeDtypeStruct((rows, width), BF16),
        scratch_shapes=[
            pltpu.VMEM((rows, width), BF16),
            pltpu.VMEM((blocks, rows), BF16),
            pltpu.SemaphoreType.DMA((PARTS + 1,)),
        ],
        cost_estimate=pl.CostEstimate(
            flops=2 * rows * width, bytes_accessed=4 * 2**20, transcendentals=0
        ),
        compiler_params=pltpu.CompilerParams(vmem_limit_bytes=VMEM),
        name="decode_table",
    )(outside(codes), outside(scale.T))


def select_rows(wanted, table):
    peers, slots = wanted.shape
    rows, width = table.shape
    return pl.pallas_call(
        select_kernel,
        out_shape=jax.ShapeDtypeStruct((peers, slots, width), BF16),
        scratch_shapes=[pltpu.VMEM((slots, peers), jnp.int32)],
        cost_estimate=pl.CostEstimate(
            flops=2 * peers * slots * rows * width, bytes_accessed=3 * 2**20, transcendentals=0
        ),
        compiler_params=pltpu.CompilerParams(vmem_limit_bytes=VMEM),
        name="select_rows",
    )(wanted, table)


def layer(live, *arrays):
    summed, _, rows, _ = arrays
    width, targets = summed.shape
    cold = rows.shape[0] * rows.shape[1]
    near = pl.BlockSpec(memory_space=pltpu.VMEM)
    return pl.pallas_call(
        layer_kernel,
        in_specs=[pl.BlockSpec(memory_space=pltpu.SMEM)] + [near] * len(arrays),
        out_specs=[pl.BlockSpec(memory_space=pltpu.HBM), near],
        out_shape=[
            jax.ShapeDtypeStruct((targets, width), BF16),
            jax.ShapeDtypeStruct((2 * width, width), BF16),
        ],
        scratch_shapes=[
            pltpu.VMEM((width + STEP, cold), BF16),
            pltpu.VMEM((targets, width), BF16),
            pltpu.SemaphoreType.DMA,
        ],
        cost_estimate=pl.CostEstimate(
            flops=2 * targets * width * (cold + 4 * width),
            bytes_accessed=5 * 2**20,
            transcendentals=targets * width,
        ),
        compiler_params=pltpu.CompilerParams(vmem_limit_bytes=VMEM),
        name="layer",
    )(live, *map(inside, arrays))


def exchange(parts, axes):
    return lax.all_to_all(parts, axes, split_axis=0, concat_axis=0, tiled=True)


def sum_everywhere(grads):
    rows, width = grads.shape
    plane = ("grp", "own")
    peers = lax.axis_size("grp") * lax.axis_size("own")
    depth = lax.axis_size("rep")
    parts = exchange(grads.reshape(peers, rows // peers, width), plane)
    share = jnp.sum(parts.astype(F32), axis=0)
    shares = exchange(jnp.broadcast_to(share[None], (depth,) + share.shape), "rep")
    share = jnp.sum(shares, axis=0).astype(BF16)
    parts = exchange(jnp.broadcast_to(share[None], (peers,) + share.shape), plane)
    return parts.reshape(rows, width).astype(F32)


def body(
    self_feat,
    neighbor,
    grad_out,
    fetch_rows,
    fetch_count,
    table_codes,
    table_scale,
    hot_table,
    self_weight,
    neighbor_weight,
):
    width = self_feat.shape[1]
    wanted = exchange(fetch_rows, "own")
    table = decode_table(table_codes, table_scale)
    summed, words, held = count_rows(
        neighbor, hot_table, self_feat, grad_out, self_weight, neighbor_weight
    )
    rows = exchange(select_rows(wanted, table), "own")
    hidden, grads = layer(fetch_count, summed, words, rows, held)
    total = sum_everywhere(grads)
    return hidden, total[:width], total[width:]


def solution(mesh):
    split = P(("grp", "own", "rep"), None)
    in_specs = (
        split,
        split,
        split,
        split,
        P(("grp", "own", "rep")),
        P("own", None),
        P("own", None),
        P(),
        P(),
        P(),
    )
    out_specs = (split, P(), P())
    return jax.shard_map(body, mesh=mesh, in_specs=in_specs, out_specs=out_specs, check_vma=False)
```

```python
import jax
import jax.numpy as jnp
from jax import lax
from jax.experimental import pallas as pl
from jax.experimental.pallas import tpu as pltpu
from jax.sharding import PartitionSpec as P

F32 = jnp.float32
BF16 = jnp.bfloat16
LANES = 128
STEP = 32
PEERS = 4
PARTS = 4
VMEM = 32 * 2**20


def counter(words, i):
    if i:
        words = lax.shift_right_logical(words, 4 * i)
    if i < 7:
        words = jnp.bitwise_and(words, 15)
    return words.astype(F32).astype(BF16)


def count_kernel(
    nbr_ref,
    hot_hbm,
    self_hbm,
    grad_hbm,
    self_w_hbm,
    nbr_w_hbm,
    sum_ref,
    cold_ref,
    held_ref,
    grad_ref,
    hot_ref,
    keys_ref,
    counts_ref,
    sems,
):
    moves = [(hot_hbm, hot_ref), (grad_hbm, grad_ref)]
    start = 0
    for array in (self_hbm, self_w_hbm, nbr_w_hbm):
        moves.append((array, held_ref.at[start : start + array.shape[0]]))
        start += array.shape[0]
    copies = [pltpu.make_async_copy(*move, sems.at[i]) for i, move in enumerate(moves)]
    for copy in copies:
        copy.start()
    targets = nbr_ref.shape[1]
    hot_blocks = hot_ref.shape[0] // LANES
    groups = hot_blocks // 8 + 1
    steps = LANES // STEP

    neighbors = nbr_ref.shape[0]
    picks = nbr_ref[...]
    keys_ref[0, :neighbors, :] = jnp.bitwise_and(picks, LANES - 1)
    bit = jnp.left_shift(jnp.int32(1), jnp.bitwise_and(jnp.right_shift(picks, 5), 28))
    group = jnp.right_shift(picks, 10)
    for g in range(groups):
        keys_ref[1 + g, :neighbors, :] = jnp.where(group == g, bit, 0)

    def step(i, carry):
        cut = pl.ds(pl.multiple_of((i // steps) * LANES, LANES), LANES)
        base = pl.multiple_of((i % steps) * STEP, STEP)
        place = lax.broadcasted_iota(jnp.int32, (STEP, LANES), 0) + base
        words = [jnp.zeros((STEP, LANES), jnp.int32) for _ in range(groups)]
        for k in range(neighbors):
            spread = lambda r: jnp.broadcast_to(keys_ref[r, k : k + 1, cut], (STEP, LANES))
            here = spread(0) == place
            for g in range(groups):
                words[g] = words[g] + jnp.where(here, spread(1 + g), 0)
        for b in range(hot_blocks):
            counts_ref[pl.ds(b * LANES + base, STEP), cut] = counter(words[b // 8], b % 8)
        cold_ref[pl.ds(base, STEP), cut] = words[groups - 1]
        return carry

    lax.fori_loop(0, (targets // LANES) * steps, step, 0)
    for copy in copies:
        copy.wait()
    sum_ref[...] = held_ref[:targets, :].astype(F32).T + lax.dot_general(
        hot_ref[...], counts_ref[...], (((0,), (0,)), ((), ())), preferred_element_type=F32
    )


def prepare_kernel(
    nbr_hbm, code_hbm, scale_hbm, nbr_ref, out_ref, code_ref, scale_ref, sems
):
    rows, width = code_ref.shape
    blocks = scale_ref.shape[0]
    part = rows // PARTS
    scale_copy = pltpu.make_async_copy(scale_hbm, scale_ref, sems.at[PARTS])
    scale_copy.start()
    nbr_copy = pltpu.make_async_copy(nbr_hbm, nbr_ref, sems.at[PARTS + 1])
    nbr_copy.start()
    cuts = [slice(i * part, (i + 1) * part) for i in range(PARTS)]
    copies = [
        pltpu.make_async_copy(code_hbm.at[cut], code_ref.at[cut], sems.at[i])
        for i, cut in enumerate(cuts)
    ]
    for copy in copies:
        copy.start()
    which = lax.broadcasted_iota(jnp.int32, (blocks, width), 0)
    block = lax.broadcasted_iota(jnp.int32, (blocks, width), 1) // (width // blocks)
    ones = jnp.where(which == block, 1.0, 0.0).astype(BF16)
    scale_copy.wait()
    scale = lax.dot_general(
        scale_ref[...], ones, (((0,), (0,)), ((), ())), preferred_element_type=F32
    )
    for cut, copy in zip(cuts, copies):
        copy.wait()
        out_ref[cut] = (code_ref[cut].astype(F32) * scale[cut]).astype(BF16)
    nbr_copy.wait()


def select_kernel(want_ref, table_ref, out_ref, cols_ref):
    peers, slots = want_ref.shape
    rows, width = table_ref.shape
    cols_ref[...] = want_ref[...].T
    lane = lax.broadcasted_iota(jnp.int32, (slots, rows), 1)
    for p in range(0, peers, PEERS):
        picks = [
            jnp.where(jnp.broadcast_to(cols_ref[:, q : q + 1], (slots, rows)) == lane, 1.0, 0.0)
            for q in range(p, p + PEERS)
        ]
        pick = jnp.concatenate(picks, axis=0).astype(BF16)
        found = jnp.dot(pick, table_ref[...], preferred_element_type=F32).astype(BF16)
        out_ref[p : p + PEERS] = found.reshape(PEERS, slots, width)


def layer_kernel(
    live_ref,
    sum_ref,
    words_ref,
    rows_ref,
    held_ref,
    grad_ref,
    hidden_hbm,
    grads_ref,
    cold_ref,
    hidden_ref,
    sem,
):
    owners, slots, width = rows_ref.shape
    targets = sum_ref.shape[1]
    rows = []
    for p in range(owners):
        slot = lax.broadcasted_iota(jnp.int32, (slots, width), 0)
        rows.append(jnp.where(slot < live_ref[p], rows_ref[p].astype(F32), 0.0))
    cold_ref[:width, :] = jnp.concatenate(rows, axis=0).T.astype(BF16)
    dead = [
        jnp.where(lax.broadcasted_iota(jnp.int32, (1, slots), 1) < live_ref[p], 0.0, 1.0)
        for p in range(owners)
    ]
    dead = jnp.broadcast_to(jnp.concatenate(dead, axis=1), (STEP, owners * slots))
    cold_ref[width:, :] = dead.astype(BF16)

    words = words_ref[...]
    blocks = owners * slots // LANES
    counts = jnp.concatenate([counter(words, b) for b in range(blocks)], axis=0)
    cold = jnp.dot(cold_ref[...], counts, preferred_element_type=F32)
    share = 1.0 / (16.0 - cold[width : width + 1, :])
    mean_t = ((sum_ref[...] + cold[:width, :]) * share).astype(BF16)
    mean = mean_t.T
    own = held_ref[:targets, :]
    pre = jnp.dot(own, held_ref[targets : targets + width, :], preferred_element_type=F32) + jnp.dot(
        mean, held_ref[targets + width :, :], preferred_element_type=F32
    )
    sigma = 1.0 / (1.0 + jnp.exp(-pre))
    hidden_ref[...] = (pre * sigma).astype(BF16)
    out = pltpu.make_async_copy(hidden_ref, hidden_hbm, sem)
    out.start()
    slope = sigma * (1.0 + pre * (1.0 - sigma))
    delta = (grad_ref[...].astype(F32) * slope).astype(BF16)
    across = (((0,), (0,)), ((), ()))
    grads_ref[:width, :] = lax.dot_general(
        own, delta, across, preferred_element_type=F32
    ).astype(BF16)
    grads_ref[width:, :] = jnp.dot(mean_t, delta, preferred_element_type=F32).astype(BF16)
    out.wait()


def outside(array):
    return pltpu.with_memory_space_constraint(array, pltpu.HBM)


def inside(array):
    return pltpu.with_memory_space_constraint(array, pltpu.VMEM)


def count_rows(picks, hot_table, self_feat, grad_out, self_weight, neighbor_weight):
    targets, width = self_feat.shape
    hot = hot_table.shape[0]
    arrays = (hot_table, self_feat, grad_out, self_weight, neighbor_weight)
    held = targets + self_weight.shape[0] + neighbor_weight.shape[0]
    return pl.pallas_call(
        count_kernel,
        in_specs=[pl.BlockSpec(memory_space=pltpu.VMEM)]
        + [pl.BlockSpec(memory_space=pltpu.HBM)] * len(arrays),
        out_shape=[
            jax.ShapeDtypeStruct((width, targets), F32),
            jax.ShapeDtypeStruct((LANES, targets), jnp.int32),
            jax.ShapeDtypeStruct((held, width), BF16),
            jax.ShapeDtypeStruct((targets, width), BF16),
        ],
        scratch_shapes=[
            pltpu.VMEM((hot, width), BF16),
            pltpu.VMEM((4, 16, targets), jnp.int32),
            pltpu.VMEM((hot, targets), BF16),
            pltpu.SemaphoreType.DMA((len(arrays),)),
        ],
        cost_estimate=pl.CostEstimate(
            flops=2 * targets * hot * width, bytes_accessed=16 * 2**20, transcendentals=0
        ),
        compiler_params=pltpu.CompilerParams(vmem_limit_bytes=VMEM),
        name="count_rows",
    )(picks, *map(outside, arrays))


def prepare(neighbor, codes, scale):
    rows, width = codes.shape
    blocks = scale.shape[1]
    targets, neighbors = neighbor.shape
    return pl.pallas_call(
        prepare_kernel,
        in_specs=[pl.BlockSpec(memory_space=pltpu.HBM)] * 3,
        out_shape=[
            jax.ShapeDtypeStruct((neighbors, targets), jnp.int32),
            jax.ShapeDtypeStruct((rows, width), BF16),
        ],
        scratch_shapes=[
            pltpu.VMEM((rows, width), BF16),
            pltpu.VMEM((blocks, rows), BF16),
            pltpu.SemaphoreType.DMA((PARTS + 2,)),
        ],
        cost_estimate=pl.CostEstimate(
            flops=2 * rows * width, bytes_accessed=4 * 2**20, transcendentals=0
        ),
        compiler_params=pltpu.CompilerParams(vmem_limit_bytes=VMEM),
        name="prepare",
    )(outside(neighbor.T), outside(codes), outside(scale.T))


def select_rows(wanted, table):
    peers, slots = wanted.shape
    rows, width = table.shape
    return pl.pallas_call(
        select_kernel,
        out_shape=jax.ShapeDtypeStruct((peers, slots, width), BF16),
        scratch_shapes=[pltpu.VMEM((slots, peers), jnp.int32)],
        cost_estimate=pl.CostEstimate(
            flops=2 * peers * slots * rows * width, bytes_accessed=3 * 2**20, transcendentals=0
        ),
        compiler_params=pltpu.CompilerParams(vmem_limit_bytes=VMEM),
        name="select_rows",
    )(wanted, table)


def layer(live, summed, words, rows, held, grad_out):
    width, targets = summed.shape
    cold = rows.shape[0] * rows.shape[1]
    near = pl.BlockSpec(memory_space=pltpu.VMEM)
    far = pl.BlockSpec(memory_space=pltpu.HBM)
    return pl.pallas_call(
        layer_kernel,
        in_specs=[pl.BlockSpec(memory_space=pltpu.SMEM)] + [near] * 5,
        out_specs=[far, near],
        out_shape=[
            jax.ShapeDtypeStruct((targets, width), BF16),
            jax.ShapeDtypeStruct((2 * width, width), BF16),
        ],
        scratch_shapes=[
            pltpu.VMEM((width + STEP, cold), BF16),
            pltpu.VMEM((targets, width), BF16),
            pltpu.SemaphoreType.DMA,
        ],
        cost_estimate=pl.CostEstimate(
            flops=2 * targets * width * (cold + 4 * width),
            bytes_accessed=5 * 2**20,
            transcendentals=targets * width,
        ),
        compiler_params=pltpu.CompilerParams(vmem_limit_bytes=VMEM),
        name="layer",
    )(live, *map(inside, (summed, words, rows, held, grad_out)))


def exchange(parts, axes):
    return lax.all_to_all(parts, axes, split_axis=0, concat_axis=0, tiled=True)


def sum_everywhere(grads):
    rows, width = grads.shape
    plane = ("grp", "own")
    peers = lax.axis_size("grp") * lax.axis_size("own")
    depth = lax.axis_size("rep")
    parts = exchange(grads.reshape(peers, rows // peers, width), plane)
    share = jnp.sum(parts.astype(F32), axis=0)
    shares = exchange(jnp.broadcast_to(share[None], (depth,) + share.shape), "rep")
    share = jnp.sum(shares, axis=0).astype(BF16)
    parts = exchange(jnp.broadcast_to(share[None], (peers,) + share.shape), plane)
    return parts.reshape(rows, width).astype(F32)


def body(
    self_feat,
    neighbor,
    grad_out,
    fetch_rows,
    fetch_count,
    table_codes,
    table_scale,
    hot_table,
    self_weight,
    neighbor_weight,
):
    width = self_feat.shape[1]
    wanted = exchange(fetch_rows, "own")
    picks, table = prepare(neighbor, table_codes, table_scale)
    summed, words, held, grad_out = count_rows(
        picks, hot_table, self_feat, grad_out, self_weight, neighbor_weight
    )
    rows = exchange(select_rows(wanted, table), "own")
    hidden, grads = layer(fetch_count, summed, words, rows, held, grad_out)
    total = sum_everywhere(grads)
    return hidden, total[:width], total[width:]


def solution(mesh):
    split = P(("grp", "own", "rep"), None)
    in_specs = (
        split,
        split,
        split,
        split,
        P(("grp", "own", "rep")),
        P("own", None),
        P("own", None),
        P(),
        P(),
        P(),
    )
    out_specs = (split, P(), P())
    return jax.shard_map(body, mesh=mesh, in_specs=in_specs, out_specs=out_specs, check_vma=False)
```

```python
import jax
import jax.numpy as jnp
from jax import lax
from jax.experimental import pallas as pl
from jax.experimental.pallas import tpu as pltpu
from jax.sharding import PartitionSpec as P

F32 = jnp.float32
BF16 = jnp.bfloat16
LANES = 128
STEP = 32
PEERS = 4
PARTS = 4
VMEM = 32 * 2**20


def counter(words, i):
    if i:
        words = lax.shift_right_logical(words, 4 * i)
    if i < 7:
        words = jnp.bitwise_and(words, 15)
    return words.astype(F32).astype(BF16)


def count_kernel(
    nbr_ref,
    hot_hbm,
    self_hbm,
    grad_hbm,
    self_w_hbm,
    nbr_w_hbm,
    sum_ref,
    cold_ref,
    held_ref,
    grad_ref,
    hot_ref,
    keys_ref,
    counts_ref,
    sems,
):
    moves = [(hot_hbm, hot_ref), (grad_hbm, grad_ref)]
    start = 0
    for array in (self_hbm, self_w_hbm, nbr_w_hbm):
        moves.append((array, held_ref.at[start : start + array.shape[0]]))
        start += array.shape[0]
    copies = [pltpu.make_async_copy(*move, sems.at[i]) for i, move in enumerate(moves)]
    for copy in copies:
        copy.start()
    targets = nbr_ref.shape[1]
    hot_blocks = hot_ref.shape[0] // LANES
    groups = hot_blocks // 8 + 1
    steps = LANES // STEP

    neighbors = nbr_ref.shape[0]
    picks = nbr_ref[...]
    keys_ref[0, :neighbors, :] = jnp.bitwise_and(picks, LANES - 1)
    bit = jnp.left_shift(jnp.int32(1), jnp.bitwise_and(jnp.right_shift(picks, 5), 28))
    group = jnp.right_shift(picks, 10)
    for g in range(groups):
        keys_ref[1 + g, :neighbors, :] = jnp.where(group == g, bit, 0)

    def step(i, carry):
        cut = pl.ds(pl.multiple_of((i // steps) * LANES, LANES), LANES)
        base = pl.multiple_of((i % steps) * STEP, STEP)
        place = lax.broadcasted_iota(jnp.int32, (STEP, LANES), 0) + base
        words = [jnp.zeros((STEP, LANES), jnp.int32) for _ in range(groups)]
        for k in range(neighbors):
            spread = lambda r: jnp.broadcast_to(keys_ref[r, k : k + 1, cut], (STEP, LANES))
            here = spread(0) == place
            for g in range(groups):
                words[g] = words[g] + jnp.where(here, spread(1 + g), 0)
        for b in range(hot_blocks):
            counts_ref[pl.ds(b * LANES + base, STEP), cut] = counter(words[b // 8], b % 8)
        cold_ref[pl.ds(base, STEP), cut] = words[groups - 1]
        return carry

    lax.fori_loop(0, (targets // LANES) * steps, step, 0)
    for copy in copies:
        copy.wait()
    sum_ref[...] = held_ref[:targets, :].astype(F32).T + lax.dot_general(
        hot_ref[...], counts_ref[...], (((0,), (0,)), ((), ())), preferred_element_type=F32
    )


def prepare_kernel(
    nbr_hbm, code_hbm, scale_hbm, nbr_ref, out_ref, code_ref, scale_ref, sems
):
    rows, width = code_ref.shape
    blocks = scale_ref.shape[0]
    part = rows // PARTS
    scale_copy = pltpu.make_async_copy(scale_hbm, scale_ref, sems.at[PARTS])
    scale_copy.start()
    nbr_copy = pltpu.make_async_copy(nbr_hbm, nbr_ref, sems.at[PARTS + 1])
    nbr_copy.start()
    cuts = [slice(i * part, (i + 1) * part) for i in range(PARTS)]
    copies = [
        pltpu.make_async_copy(code_hbm.at[cut], code_ref.at[cut], sems.at[i])
        for i, cut in enumerate(cuts)
    ]
    for copy in copies:
        copy.start()
    which = lax.broadcasted_iota(jnp.int32, (blocks, width), 0)
    block = lax.broadcasted_iota(jnp.int32, (blocks, width), 1) // (width // blocks)
    ones = jnp.where(which == block, 1.0, 0.0).astype(BF16)
    scale_copy.wait()
    scale = lax.dot_general(
        scale_ref[...], ones, (((0,), (0,)), ((), ())), preferred_element_type=F32
    )
    for cut, copy in zip(cuts, copies):
        copy.wait()
        out_ref[cut] = (code_ref[cut].astype(F32) * scale[cut]).astype(BF16)
    nbr_copy.wait()


def select_kernel(want_ref, table_ref, out_ref, cols_ref):
    peers, slots = want_ref.shape
    rows, width = table_ref.shape
    cols_ref[...] = want_ref[...].T
    lane = lax.broadcasted_iota(jnp.int32, (slots, rows), 1)
    for p in range(0, peers, PEERS):
        picks = [
            jnp.where(jnp.broadcast_to(cols_ref[:, q : q + 1], (slots, rows)) == lane, 1.0, 0.0)
            for q in range(p, p + PEERS)
        ]
        pick = jnp.concatenate(picks, axis=0).astype(BF16)
        found = jnp.dot(pick, table_ref[...], preferred_element_type=F32).astype(BF16)
        out_ref[p : p + PEERS] = found.reshape(PEERS, slots, width)


def layer_kernel(
    live_ref,
    sum_ref,
    words_ref,
    rows_ref,
    held_ref,
    grad_ref,
    hidden_hbm,
    grads_ref,
    cold_ref,
    hidden_ref,
    sem,
):
    owners, slots, width = rows_ref.shape
    targets = sum_ref.shape[1]
    rows = []
    for p in range(owners):
        slot = lax.broadcasted_iota(jnp.int32, (slots, width), 0)
        rows.append(jnp.where(slot < live_ref[p], rows_ref[p].astype(F32), 0.0))
    cold_ref[:width, :] = jnp.concatenate(rows, axis=0).T.astype(BF16)
    dead = [
        jnp.where(lax.broadcasted_iota(jnp.int32, (1, slots), 1) < live_ref[p], 0.0, 1.0)
        for p in range(owners)
    ]
    dead = jnp.broadcast_to(jnp.concatenate(dead, axis=1), (STEP, owners * slots))
    cold_ref[width:, :] = dead.astype(BF16)

    words = words_ref[...]
    blocks = owners * slots // LANES
    counts = jnp.concatenate([counter(words, b) for b in range(blocks)], axis=0)
    cold = jnp.dot(cold_ref[...], counts, preferred_element_type=F32)
    share = 1.0 / (16.0 - cold[width : width + 1, :])
    mean_t = ((sum_ref[...] + cold[:width, :]) * share).astype(BF16)
    mean = mean_t.T
    own = held_ref[:targets, :]
    pre = jnp.dot(own, held_ref[targets : targets + width, :], preferred_element_type=F32) + jnp.dot(
        mean, held_ref[targets + width :, :], preferred_element_type=F32
    )
    sigma = 1.0 / (1.0 + jnp.exp(-pre))
    hidden_ref[...] = (pre * sigma).astype(BF16)
    out = pltpu.make_async_copy(hidden_ref, hidden_hbm, sem)
    out.start()
    slope = sigma * (1.0 + pre * (1.0 - sigma))
    delta = (grad_ref[...].astype(F32) * slope).astype(BF16)
    across = (((0,), (0,)), ((), ()))
    grads_ref[:width, :] = lax.dot_general(
        own, delta, across, preferred_element_type=F32
    ).astype(BF16)
    grads_ref[width:, :] = jnp.dot(mean_t, delta, preferred_element_type=F32).astype(BF16)
    out.wait()


def outside(array):
    return pltpu.with_memory_space_constraint(array, pltpu.HBM)


def inside(array):
    return pltpu.with_memory_space_constraint(array, pltpu.VMEM)


def count_rows(picks, hot_table, self_feat, grad_out, self_weight, neighbor_weight):
    targets, width = self_feat.shape
    hot = hot_table.shape[0]
    arrays = (hot_table, self_feat, grad_out, self_weight, neighbor_weight)
    held = targets + self_weight.shape[0] + neighbor_weight.shape[0]
    return pl.pallas_call(
        count_kernel,
        in_specs=[pl.BlockSpec(memory_space=pltpu.VMEM)]
        + [pl.BlockSpec(memory_space=pltpu.HBM)] * len(arrays),
        out_shape=[
            jax.ShapeDtypeStruct((width, targets), F32),
            jax.ShapeDtypeStruct((LANES, targets), jnp.int32),
            jax.ShapeDtypeStruct((held, width), BF16),
            jax.ShapeDtypeStruct((targets, width), BF16),
        ],
        scratch_shapes=[
            pltpu.VMEM((hot, width), BF16),
            pltpu.VMEM((4, 16, targets), jnp.int32),
            pltpu.VMEM((hot, targets), BF16),
            pltpu.SemaphoreType.DMA((len(arrays),)),
        ],
        cost_estimate=pl.CostEstimate(
            flops=2 * targets * hot * width, bytes_accessed=16 * 2**20, transcendentals=0
        ),
        compiler_params=pltpu.CompilerParams(vmem_limit_bytes=VMEM),
        name="count_rows",
    )(picks, *map(outside, arrays))


def prepare(neighbor, codes, scale):
    rows, width = codes.shape
    blocks = scale.shape[1]
    targets, neighbors = neighbor.shape
    return pl.pallas_call(
        prepare_kernel,
        in_specs=[pl.BlockSpec(memory_space=pltpu.HBM)] * 3,
        out_shape=[
            jax.ShapeDtypeStruct((neighbors, targets), jnp.int32),
            jax.ShapeDtypeStruct((rows, width), BF16),
        ],
        scratch_shapes=[
            pltpu.VMEM((rows, width), BF16),
            pltpu.VMEM((blocks, rows), BF16),
            pltpu.SemaphoreType.DMA((PARTS + 2,)),
        ],
        cost_estimate=pl.CostEstimate(
            flops=2 * rows * width, bytes_accessed=4 * 2**20, transcendentals=0
        ),
        compiler_params=pltpu.CompilerParams(vmem_limit_bytes=VMEM),
        name="prepare",
    )(outside(neighbor.T), outside(codes), outside(scale.T))


def select_rows(wanted, table):
    peers, slots = wanted.shape
    rows, width = table.shape
    return pl.pallas_call(
        select_kernel,
        out_shape=jax.ShapeDtypeStruct((peers, slots, width), BF16),
        scratch_shapes=[pltpu.VMEM((slots, peers), jnp.int32)],
        cost_estimate=pl.CostEstimate(
            flops=2 * peers * slots * rows * width, bytes_accessed=3 * 2**20, transcendentals=0
        ),
        compiler_params=pltpu.CompilerParams(vmem_limit_bytes=VMEM),
        name="select_rows",
    )(wanted, table)


def layer(live, summed, words, rows, held, grad_out):
    width, targets = summed.shape
    cold = rows.shape[0] * rows.shape[1]
    near = pl.BlockSpec(memory_space=pltpu.VMEM)
    far = pl.BlockSpec(memory_space=pltpu.HBM)
    return pl.pallas_call(
        layer_kernel,
        in_specs=[pl.BlockSpec(memory_space=pltpu.SMEM)] + [near] * 5,
        out_specs=[far, near],
        out_shape=[
            jax.ShapeDtypeStruct((targets, width), BF16),
            jax.ShapeDtypeStruct((2 * width, width), BF16),
        ],
        scratch_shapes=[
            pltpu.VMEM((width + STEP, cold), BF16),
            pltpu.VMEM((targets, width), BF16),
            pltpu.SemaphoreType.DMA,
        ],
        cost_estimate=pl.CostEstimate(
            flops=2 * targets * width * (cold + 4 * width),
            bytes_accessed=5 * 2**20,
            transcendentals=targets * width,
        ),
        compiler_params=pltpu.CompilerParams(vmem_limit_bytes=VMEM),
        name="layer",
    )(live, *map(inside, (summed, words, rows, held, grad_out)))


def exchange(parts, axes):
    return lax.all_to_all(parts, axes, split_axis=0, concat_axis=0, tiled=True)


def sum_everywhere(grads):
    rows, width = grads.shape
    plane = ("grp", "own")
    peers = lax.axis_size("grp") * lax.axis_size("own")
    depth = lax.axis_size("rep")
    parts = exchange(grads.reshape(peers, rows // peers, width), plane)
    share = jnp.sum(parts.astype(F32), axis=0).astype(BF16)
    shares = exchange(jnp.broadcast_to(share[None], (depth,) + share.shape), "rep")
    share = jnp.sum(shares.astype(F32), axis=0).astype(BF16)
    parts = exchange(jnp.broadcast_to(share[None], (peers,) + share.shape), plane)
    return parts.reshape(rows, width).astype(F32)


def body(
    self_feat,
    neighbor,
    grad_out,
    fetch_rows,
    fetch_count,
    table_codes,
    table_scale,
    hot_table,
    self_weight,
    neighbor_weight,
):
    width = self_feat.shape[1]
    wanted = exchange(fetch_rows, "own")
    picks, table = prepare(neighbor, table_codes, table_scale)
    summed, words, held, grad_out = count_rows(
        picks, hot_table, self_feat, grad_out, self_weight, neighbor_weight
    )
    rows = exchange(select_rows(wanted, table), "own")
    hidden, grads = layer(fetch_count, summed, words, rows, held, grad_out)
    total = sum_everywhere(grads)
    return hidden, total[:width], total[width:]


def solution(mesh):
    split = P(("grp", "own", "rep"), None)
    in_specs = (
        split,
        split,
        split,
        split,
        P(("grp", "own", "rep")),
        P("own", None),
        P("own", None),
        P(),
        P(),
        P(),
    )
    out_specs = (split, P(), P())
    return jax.shard_map(body, mesh=mesh, in_specs=in_specs, out_specs=out_specs, check_vma=False)
```

```python
import jax
import jax.numpy as jnp
from jax import lax
from jax.experimental import pallas as pl
from jax.experimental.pallas import tpu as pltpu
from jax.sharding import PartitionSpec as P

F32 = jnp.float32
BF16 = jnp.bfloat16
LANES = 128
STEP = 32
PEERS = 4
PARTS = 4
CHUNKS = 2
VMEM = 32 * 2**20


def counter(words, i):
    if i:
        words = lax.shift_right_logical(words, 4 * i)
    if i < 7:
        words = jnp.bitwise_and(words, 15)
    return words.astype(F32).astype(BF16)


def count_kernel(
    nbr_ref,
    hot_hbm,
    self_hbm,
    grad_hbm,
    self_w_hbm,
    nbr_w_hbm,
    sum_ref,
    cold_ref,
    held_ref,
    grad_ref,
    hot_ref,
    keys_ref,
    counts_ref,
    sems,
):
    moves = [(hot_hbm, hot_ref), (grad_hbm, grad_ref)]
    start = 0
    for array in (self_hbm, self_w_hbm, nbr_w_hbm):
        moves.append((array, held_ref.at[start : start + array.shape[0]]))
        start += array.shape[0]
    copies = [pltpu.make_async_copy(*move, sems.at[i]) for i, move in enumerate(moves)]
    for copy in copies:
        copy.start()
    targets = nbr_ref.shape[1]
    hot_blocks = hot_ref.shape[0] // LANES
    groups = hot_blocks // 8 + 1
    steps = LANES // STEP

    neighbors = nbr_ref.shape[0]
    picks = nbr_ref[...]
    keys_ref[0, :neighbors, :] = jnp.bitwise_and(picks, LANES - 1)
    bit = jnp.left_shift(jnp.int32(1), jnp.bitwise_and(jnp.right_shift(picks, 5), 28))
    group = jnp.right_shift(picks, 10)
    for g in range(groups):
        keys_ref[1 + g, :neighbors, :] = jnp.where(group == g, bit, 0)

    def step(i, carry):
        cut = pl.ds(pl.multiple_of((i // steps) * LANES, LANES), LANES)
        base = pl.multiple_of((i % steps) * STEP, STEP)
        place = lax.broadcasted_iota(jnp.int32, (STEP, LANES), 0) + base
        words = [jnp.zeros((STEP, LANES), jnp.int32) for _ in range(groups)]
        for k in range(neighbors):
            spread = lambda r: jnp.broadcast_to(keys_ref[r, k : k + 1, cut], (STEP, LANES))
            here = spread(0) == place
            for g in range(groups):
                words[g] = words[g] + jnp.where(here, spread(1 + g), 0)
        for b in range(hot_blocks):
            counts_ref[pl.ds(b * LANES + base, STEP), cut] = counter(words[b // 8], b % 8)
        cold_ref[pl.ds(base, STEP), cut] = words[groups - 1]
        return carry

    lax.fori_loop(0, (targets // LANES) * steps, step, 0)
    for copy in copies:
        copy.wait()
    sum_ref[...] = held_ref[:targets, :].astype(F32).T + lax.dot_general(
        hot_ref[...], counts_ref[...], (((0,), (0,)), ((), ())), preferred_element_type=F32
    )


def prepare_kernel(
    nbr_hbm, code_hbm, scale_hbm, nbr_ref, out_ref, code_ref, scale_ref, sems
):
    rows, width = code_ref.shape
    blocks = scale_ref.shape[0]
    part = rows // PARTS
    scale_copy = pltpu.make_async_copy(scale_hbm, scale_ref, sems.at[PARTS])
    scale_copy.start()
    nbr_copy = pltpu.make_async_copy(nbr_hbm, nbr_ref, sems.at[PARTS + 1])
    nbr_copy.start()
    cuts = [slice(i * part, (i + 1) * part) for i in range(PARTS)]
    copies = [
        pltpu.make_async_copy(code_hbm.at[cut], code_ref.at[cut], sems.at[i])
        for i, cut in enumerate(cuts)
    ]
    for copy in copies:
        copy.start()
    which = lax.broadcasted_iota(jnp.int32, (blocks, width), 0)
    block = lax.broadcasted_iota(jnp.int32, (blocks, width), 1) // (width // blocks)
    ones = jnp.where(which == block, 1.0, 0.0).astype(BF16)
    scale_copy.wait()
    scale = lax.dot_general(
        scale_ref[...], ones, (((0,), (0,)), ((), ())), preferred_element_type=F32
    )
    for cut, copy in zip(cuts, copies):
        copy.wait()
        out_ref[cut] = (code_ref[cut].astype(F32) * scale[cut]).astype(BF16)
    nbr_copy.wait()


def select_kernel(want_ref, table_ref, out_ref, cols_ref):
    peers, slots = want_ref.shape
    rows, width = table_ref.shape
    cols_ref[...] = want_ref[...].T
    lane = lax.broadcasted_iota(jnp.int32, (slots, rows), 1)
    for p in range(0, peers, PEERS):
        picks = [
            jnp.where(jnp.broadcast_to(cols_ref[:, q : q + 1], (slots, rows)) == lane, 1.0, 0.0)
            for q in range(p, p + PEERS)
        ]
        pick = jnp.concatenate(picks, axis=0).astype(BF16)
        found = jnp.dot(pick, table_ref[...], preferred_element_type=F32).astype(BF16)
        out_ref[p : p + PEERS] = found.reshape(PEERS, slots, width)


def layer_kernel(
    live_ref,
    sum_ref,
    words_ref,
    rows_ref,
    held_ref,
    grad_ref,
    hidden_hbm,
    grads_ref,
    cold_ref,
    hidden_ref,
    sems,
):
    owners, slots, width = rows_ref.shape
    targets = sum_ref.shape[1]
    rows = []
    for p in range(owners):
        slot = lax.broadcasted_iota(jnp.int32, (slots, width), 0)
        rows.append(jnp.where(slot < live_ref[p], rows_ref[p].astype(F32), 0.0))
    cold_ref[:width, :] = jnp.concatenate(rows, axis=0).astype(BF16).T
    dead = [
        jnp.where(lax.broadcasted_iota(jnp.int32, (1, slots), 1) < live_ref[p], 0.0, 1.0)
        for p in range(owners)
    ]
    dead = jnp.broadcast_to(jnp.concatenate(dead, axis=1), (STEP, owners * slots))
    cold_ref[width:, :] = dead.astype(BF16)

    blocks = owners * slots // LANES
    part = targets // CHUNKS
    outs = []
    own_sum = mean_sum = None
    for i in range(CHUNKS):
        cut = slice(i * part, (i + 1) * part)
        words = words_ref[:, cut]
        counts = jnp.concatenate([counter(words, b) for b in range(blocks)], axis=0)
        cold = jnp.dot(cold_ref[...], counts, preferred_element_type=F32)
        share = 1.0 / (16.0 - cold[width : width + 1, :])
        mean_t = ((sum_ref[:, cut] + cold[:width, :]) * share).astype(BF16)
        mean = mean_t.T
        own = held_ref[cut, :]
        both = jnp.concatenate([own, mean], axis=1)
        pre = jnp.dot(both, held_ref[targets:, :], preferred_element_type=F32)
        sigma = 1.0 / (1.0 + jnp.exp(-pre))
        hidden_ref[cut, :] = (pre * sigma).astype(BF16)
        outs.append(pltpu.make_async_copy(hidden_ref.at[cut], hidden_hbm.at[cut], sems.at[i]))
        outs[-1].start()
        slope = sigma * (1.0 + pre * (1.0 - sigma))
        delta = (grad_ref[cut, :].astype(F32) * slope).astype(BF16)
        across = (((0,), (0,)), ((), ()))
        own_part = lax.dot_general(own, delta, across, preferred_element_type=F32)
        mean_part = jnp.dot(mean_t, delta, preferred_element_type=F32)
        own_sum = own_part if i == 0 else own_sum + own_part
        mean_sum = mean_part if i == 0 else mean_sum + mean_part
    grads_ref[:width, :] = own_sum.astype(BF16)
    grads_ref[width:, :] = mean_sum.astype(BF16)
    for out in outs:
        out.wait()


def outside(array):
    return pltpu.with_memory_space_constraint(array, pltpu.HBM)


def inside(array):
    return pltpu.with_memory_space_constraint(array, pltpu.VMEM)


def count_rows(picks, hot_table, self_feat, grad_out, self_weight, neighbor_weight):
    targets, width = self_feat.shape
    hot = hot_table.shape[0]
    arrays = (hot_table, self_feat, grad_out, self_weight, neighbor_weight)
    held = targets + self_weight.shape[0] + neighbor_weight.shape[0]
    return pl.pallas_call(
        count_kernel,
        in_specs=[pl.BlockSpec(memory_space=pltpu.VMEM)]
        + [pl.BlockSpec(memory_space=pltpu.HBM)] * len(arrays),
        out_shape=[
            jax.ShapeDtypeStruct((width, targets), F32),
            jax.ShapeDtypeStruct((LANES, targets), jnp.int32),
            jax.ShapeDtypeStruct((held, width), BF16),
            jax.ShapeDtypeStruct((targets, width), BF16),
        ],
        scratch_shapes=[
            pltpu.VMEM((hot, width), BF16),
            pltpu.VMEM((4, 16, targets), jnp.int32),
            pltpu.VMEM((hot, targets), BF16),
            pltpu.SemaphoreType.DMA((len(arrays),)),
        ],
        cost_estimate=pl.CostEstimate(
            flops=2 * targets * hot * width, bytes_accessed=16 * 2**20, transcendentals=0
        ),
        compiler_params=pltpu.CompilerParams(vmem_limit_bytes=VMEM),
        name="count_rows",
    )(picks, *map(outside, arrays))


def prepare(neighbor, codes, scale):
    rows, width = codes.shape
    blocks = scale.shape[1]
    targets, neighbors = neighbor.shape
    return pl.pallas_call(
        prepare_kernel,
        in_specs=[pl.BlockSpec(memory_space=pltpu.HBM)] * 3,
        out_shape=[
            jax.ShapeDtypeStruct((neighbors, targets), jnp.int32),
            jax.ShapeDtypeStruct((rows, width), BF16),
        ],
        scratch_shapes=[
            pltpu.VMEM((rows, width), BF16),
            pltpu.VMEM((blocks, rows), BF16),
            pltpu.SemaphoreType.DMA((PARTS + 2,)),
        ],
        cost_estimate=pl.CostEstimate(
            flops=2 * rows * width, bytes_accessed=4 * 2**20, transcendentals=0
        ),
        compiler_params=pltpu.CompilerParams(vmem_limit_bytes=VMEM),
        name="prepare",
    )(outside(neighbor.T), outside(codes), outside(scale.T))


def select_rows(wanted, table):
    peers, slots = wanted.shape
    rows, width = table.shape
    return pl.pallas_call(
        select_kernel,
        out_shape=jax.ShapeDtypeStruct((peers, slots, width), BF16),
        scratch_shapes=[pltpu.VMEM((slots, peers), jnp.int32)],
        cost_estimate=pl.CostEstimate(
            flops=2 * peers * slots * rows * width, bytes_accessed=3 * 2**20, transcendentals=0
        ),
        compiler_params=pltpu.CompilerParams(vmem_limit_bytes=VMEM),
        name="select_rows",
    )(wanted, table)


def layer(live, summed, words, rows, held, grad_out):
    width, targets = summed.shape
    cold = rows.shape[0] * rows.shape[1]
    near = pl.BlockSpec(memory_space=pltpu.VMEM)
    far = pl.BlockSpec(memory_space=pltpu.HBM)
    return pl.pallas_call(
        layer_kernel,
        in_specs=[pl.BlockSpec(memory_space=pltpu.SMEM)] + [near] * 5,
        out_specs=[far, near],
        out_shape=[
            jax.ShapeDtypeStruct((targets, width), BF16),
            jax.ShapeDtypeStruct((2 * width, width), BF16),
        ],
        scratch_shapes=[
            pltpu.VMEM((width + STEP, cold), BF16),
            pltpu.VMEM((targets, width), BF16),
            pltpu.SemaphoreType.DMA((CHUNKS,)),
        ],
        cost_estimate=pl.CostEstimate(
            flops=2 * targets * width * (cold + 4 * width),
            bytes_accessed=5 * 2**20,
            transcendentals=targets * width,
        ),
        compiler_params=pltpu.CompilerParams(vmem_limit_bytes=VMEM),
        name="layer",
    )(live, *map(inside, (summed, words, rows, held, grad_out)))


def exchange(parts, axes):
    return lax.all_to_all(parts, axes, split_axis=0, concat_axis=0, tiled=True)


def sum_everywhere(grads):
    rows, width = grads.shape
    plane = ("grp", "own")
    peers = lax.axis_size("grp") * lax.axis_size("own")
    depth = lax.axis_size("rep")
    parts = exchange(grads.reshape(peers, rows // peers, width), plane)
    share = jnp.sum(parts.astype(F32), axis=0).astype(BF16)
    shares = exchange(jnp.broadcast_to(share[None], (depth,) + share.shape), "rep")
    share = jnp.sum(shares.astype(F32), axis=0).astype(BF16)
    parts = exchange(jnp.broadcast_to(share[None], (peers,) + share.shape), plane)
    return parts.reshape(rows, width).astype(F32)


def body(
    self_feat,
    neighbor,
    grad_out,
    fetch_rows,
    fetch_count,
    table_codes,
    table_scale,
    hot_table,
    self_weight,
    neighbor_weight,
):
    width = self_feat.shape[1]
    wanted = exchange(fetch_rows, "own")
    picks, table = prepare(neighbor, table_codes, table_scale)
    summed, words, held, grad_out = count_rows(
        picks, hot_table, self_feat, grad_out, self_weight, neighbor_weight
    )
    rows = exchange(select_rows(wanted, table), "own")
    hidden, grads = layer(fetch_count, summed, words, rows, held, grad_out)
    total = sum_everywhere(grads)
    return hidden, total[:width], total[width:]


def solution(mesh):
    split = P(("grp", "own", "rep"), None)
    in_specs = (
        split,
        split,
        split,
        split,
        P(("grp", "own", "rep")),
        P("own", None),
        P("own", None),
        P(),
        P(),
        P(),
    )
    out_specs = (split, P(), P())
    return jax.shard_map(body, mesh=mesh, in_specs=in_specs, out_specs=out_specs, check_vma=False)
```

```python
import jax
import jax.numpy as jnp
from jax import lax
from jax.experimental import pallas as pl
from jax.experimental.pallas import tpu as pltpu
from jax.sharding import PartitionSpec as P

F32 = jnp.float32
BF16 = jnp.bfloat16
LANES = 128
STEP = 32
PEERS = 4
PARTS = 4
CHUNKS = 2
VMEM = 32 * 2**20


def counter(words, i):
    if i:
        words = lax.shift_right_logical(words, 4 * i)
    if i < 7:
        words = jnp.bitwise_and(words, 15)
    return words.astype(F32).astype(BF16)


def count_kernel(
    nbr_ref,
    hot_hbm,
    self_hbm,
    grad_hbm,
    self_w_hbm,
    nbr_w_hbm,
    sum_ref,
    cold_ref,
    held_ref,
    grad_ref,
    hot_ref,
    keys_ref,
    counts_ref,
    sems,
):
    moves = [(hot_hbm, hot_ref), (grad_hbm, grad_ref)]
    start = 0
    for array in (self_hbm, self_w_hbm, nbr_w_hbm):
        moves.append((array, held_ref.at[start : start + array.shape[0]]))
        start += array.shape[0]
    copies = [pltpu.make_async_copy(*move, sems.at[i]) for i, move in enumerate(moves)]
    for copy in copies:
        copy.start()
    targets = nbr_ref.shape[1]
    hot_blocks = hot_ref.shape[0] // LANES
    groups = hot_blocks // 8 + 1
    steps = LANES // STEP

    neighbors = nbr_ref.shape[0]
    picks = nbr_ref[...]
    keys_ref[0, :neighbors, :] = jnp.bitwise_and(picks, LANES - 1)
    bit = jnp.left_shift(jnp.int32(1), jnp.bitwise_and(jnp.right_shift(picks, 5), 28))
    group = jnp.right_shift(picks, 10)
    for g in range(groups):
        keys_ref[1 + g, :neighbors, :] = jnp.where(group == g, bit, 0)

    def step(i, carry):
        cut = pl.ds(pl.multiple_of((i // steps) * LANES, LANES), LANES)
        base = pl.multiple_of((i % steps) * STEP, STEP)
        place = lax.broadcasted_iota(jnp.int32, (STEP, LANES), 0) + base
        words = [jnp.zeros((STEP, LANES), jnp.int32) for _ in range(groups)]
        for k in range(neighbors):
            spread = lambda r: jnp.broadcast_to(keys_ref[r, k : k + 1, cut], (STEP, LANES))
            here = spread(0) == place
            for g in range(groups):
                words[g] = words[g] + jnp.where(here, spread(1 + g), 0)
        for b in range(hot_blocks):
            counts_ref[pl.ds(b * LANES + base, STEP), cut] = counter(words[b // 8], b % 8)
        cold_ref[pl.ds(base, STEP), cut] = words[groups - 1]
        return carry

    lax.fori_loop(0, (targets // LANES) * steps, step, 0)
    for copy in copies:
        copy.wait()
    sum_ref[...] = held_ref[:targets, :].astype(F32).T + lax.dot_general(
        hot_ref[...], counts_ref[...], (((0,), (0,)), ((), ())), preferred_element_type=F32
    )


def prepare_kernel(
    nbr_hbm, code_hbm, scale_hbm, nbr_ref, out_ref, code_ref, scale_ref, sems
):
    rows, width = code_ref.shape
    blocks = scale_ref.shape[0]
    part = rows // PARTS
    scale_copy = pltpu.make_async_copy(scale_hbm, scale_ref, sems.at[PARTS])
    scale_copy.start()
    nbr_copy = pltpu.make_async_copy(nbr_hbm, nbr_ref, sems.at[PARTS + 1])
    nbr_copy.start()
    cuts = [slice(i * part, (i + 1) * part) for i in range(PARTS)]
    copies = [
        pltpu.make_async_copy(code_hbm.at[cut], code_ref.at[cut], sems.at[i])
        for i, cut in enumerate(cuts)
    ]
    for copy in copies:
        copy.start()
    which = lax.broadcasted_iota(jnp.int32, (blocks, width), 0)
    block = lax.broadcasted_iota(jnp.int32, (blocks, width), 1) // (width // blocks)
    ones = jnp.where(which == block, 1.0, 0.0).astype(BF16)
    scale_copy.wait()
    scale = lax.dot_general(
        scale_ref[...], ones, (((0,), (0,)), ((), ())), preferred_element_type=F32
    )
    for cut, copy in zip(cuts, copies):
        copy.wait()
        out_ref[cut] = (code_ref[cut].astype(F32) * scale[cut]).astype(BF16)
    nbr_copy.wait()


def select_kernel(want_ref, table_ref, out_ref, cols_ref):
    peers, slots = want_ref.shape
    rows, width = table_ref.shape
    cols_ref[...] = want_ref[...].T
    lane = lax.broadcasted_iota(jnp.int32, (slots, rows), 1)
    for p in range(0, peers, PEERS):
        picks = [
            jnp.where(jnp.broadcast_to(cols_ref[:, q : q + 1], (slots, rows)) == lane, 1.0, 0.0)
            for q in range(p, p + PEERS)
        ]
        pick = jnp.concatenate(picks, axis=0).astype(BF16)
        found = jnp.dot(pick, table_ref[...], preferred_element_type=F32).astype(BF16)
        out_ref[p : p + PEERS] = found.reshape(PEERS, slots, width)


def layer_kernel(
    live_ref,
    sum_ref,
    words_ref,
    rows_ref,
    held_ref,
    grad_ref,
    hidden_hbm,
    grads_ref,
    cold_ref,
    hidden_ref,
    sems,
):
    owners, slots, width = rows_ref.shape
    targets = sum_ref.shape[1]
    rows = []
    for p in range(owners):
        slot = lax.broadcasted_iota(jnp.int32, (slots, width), 0)
        rows.append(jnp.where(slot < live_ref[p], rows_ref[p].astype(F32), 0.0))
    cold_ref[:width, :] = jnp.concatenate(rows, axis=0).astype(BF16).T
    dead = [
        jnp.where(lax.broadcasted_iota(jnp.int32, (1, slots), 1) < live_ref[p], 0.0, 1.0)
        for p in range(owners)
    ]
    dead = jnp.broadcast_to(jnp.concatenate(dead, axis=1), (STEP, owners * slots))
    cold_ref[width:, :] = dead.astype(BF16)

    blocks = owners * slots // LANES
    part = targets // CHUNKS
    outs = []
    own_sum = mean_sum = None
    for i in range(CHUNKS):
        cut = slice(i * part, (i + 1) * part)
        words = words_ref[:, cut]
        counts = jnp.concatenate([counter(words, b) for b in range(blocks)], axis=0)
        cold = jnp.dot(cold_ref[...], counts, preferred_element_type=F32)
        share = 1.0 / (16.0 - cold[width : width + 1, :])
        mean_t = ((sum_ref[:, cut] + cold[:width, :]) * share).astype(BF16)
        mean = mean_t.T
        own = held_ref[cut, :]
        both = jnp.concatenate([own, mean], axis=1)
        pre = jnp.dot(both, held_ref[targets:, :], preferred_element_type=F32)
        sigma = 0.5 + 0.5 * jnp.tanh(0.5 * pre)
        hidden_ref[cut, :] = (pre * sigma).astype(BF16)
        outs.append(pltpu.make_async_copy(hidden_ref.at[cut], hidden_hbm.at[cut], sems.at[i]))
        outs[-1].start()
        slope = sigma * (1.0 + pre * (1.0 - sigma))
        delta = (grad_ref[cut, :].astype(F32) * slope).astype(BF16)
        across = (((0,), (0,)), ((), ()))
        own_part = lax.dot_general(own, delta, across, preferred_element_type=F32)
        mean_part = jnp.dot(mean_t, delta, preferred_element_type=F32)
        own_sum = own_part if i == 0 else own_sum + own_part
        mean_sum = mean_part if i == 0 else mean_sum + mean_part
    grads_ref[:width, :] = own_sum.astype(BF16)
    grads_ref[width:, :] = mean_sum.astype(BF16)
    for out in outs:
        out.wait()


def outside(array):
    return pltpu.with_memory_space_constraint(array, pltpu.HBM)


def inside(array):
    return pltpu.with_memory_space_constraint(array, pltpu.VMEM)


def count_rows(picks, hot_table, self_feat, grad_out, self_weight, neighbor_weight):
    targets, width = self_feat.shape
    hot = hot_table.shape[0]
    arrays = (hot_table, self_feat, grad_out, self_weight, neighbor_weight)
    held = targets + self_weight.shape[0] + neighbor_weight.shape[0]
    return pl.pallas_call(
        count_kernel,
        in_specs=[pl.BlockSpec(memory_space=pltpu.VMEM)]
        + [pl.BlockSpec(memory_space=pltpu.HBM)] * len(arrays),
        out_shape=[
            jax.ShapeDtypeStruct((width, targets), F32),
            jax.ShapeDtypeStruct((LANES, targets), jnp.int32),
            jax.ShapeDtypeStruct((held, width), BF16),
            jax.ShapeDtypeStruct((targets, width), BF16),
        ],
        scratch_shapes=[
            pltpu.VMEM((hot, width), BF16),
            pltpu.VMEM((4, 16, targets), jnp.int32),
            pltpu.VMEM((hot, targets), BF16),
            pltpu.SemaphoreType.DMA((len(arrays),)),
        ],
        cost_estimate=pl.CostEstimate(
            flops=2 * targets * hot * width, bytes_accessed=16 * 2**20, transcendentals=0
        ),
        compiler_params=pltpu.CompilerParams(vmem_limit_bytes=VMEM),
        name="count_rows",
    )(picks, *map(outside, arrays))


def prepare(neighbor, codes, scale):
    rows, width = codes.shape
    blocks = scale.shape[1]
    targets, neighbors = neighbor.shape
    return pl.pallas_call(
        prepare_kernel,
        in_specs=[pl.BlockSpec(memory_space=pltpu.HBM)] * 3,
        out_shape=[
            jax.ShapeDtypeStruct((neighbors, targets), jnp.int32),
            jax.ShapeDtypeStruct((rows, width), BF16),
        ],
        scratch_shapes=[
            pltpu.VMEM((rows, width), BF16),
            pltpu.VMEM((blocks, rows), BF16),
            pltpu.SemaphoreType.DMA((PARTS + 2,)),
        ],
        cost_estimate=pl.CostEstimate(
            flops=2 * rows * width, bytes_accessed=4 * 2**20, transcendentals=0
        ),
        compiler_params=pltpu.CompilerParams(vmem_limit_bytes=VMEM),
        name="prepare",
    )(outside(neighbor.T), outside(codes), outside(scale.T))


def select_rows(wanted, table):
    peers, slots = wanted.shape
    rows, width = table.shape
    return pl.pallas_call(
        select_kernel,
        out_shape=jax.ShapeDtypeStruct((peers, slots, width), BF16),
        scratch_shapes=[pltpu.VMEM((slots, peers), jnp.int32)],
        cost_estimate=pl.CostEstimate(
            flops=2 * peers * slots * rows * width, bytes_accessed=3 * 2**20, transcendentals=0
        ),
        compiler_params=pltpu.CompilerParams(vmem_limit_bytes=VMEM),
        name="select_rows",
    )(wanted, table)


def layer(live, summed, words, rows, held, grad_out):
    width, targets = summed.shape
    cold = rows.shape[0] * rows.shape[1]
    near = pl.BlockSpec(memory_space=pltpu.VMEM)
    far = pl.BlockSpec(memory_space=pltpu.HBM)
    return pl.pallas_call(
        layer_kernel,
        in_specs=[pl.BlockSpec(memory_space=pltpu.SMEM)] + [near] * 5,
        out_specs=[far, near],
        out_shape=[
            jax.ShapeDtypeStruct((targets, width), BF16),
            jax.ShapeDtypeStruct((2 * width, width), BF16),
        ],
        scratch_shapes=[
            pltpu.VMEM((width + STEP, cold), BF16),
            pltpu.VMEM((targets, width), BF16),
            pltpu.SemaphoreType.DMA((CHUNKS,)),
        ],
        cost_estimate=pl.CostEstimate(
            flops=2 * targets * width * (cold + 4 * width),
            bytes_accessed=5 * 2**20,
            transcendentals=targets * width,
        ),
        compiler_params=pltpu.CompilerParams(vmem_limit_bytes=VMEM),
        name="layer",
    )(live, *map(inside, (summed, words, rows, held, grad_out)))


def exchange(parts, axes):
    return lax.all_to_all(parts, axes, split_axis=0, concat_axis=0, tiled=True)


def sum_everywhere(grads):
    rows, width = grads.shape
    plane = ("grp", "own")
    peers = lax.axis_size("grp") * lax.axis_size("own")
    depth = lax.axis_size("rep")
    parts = exchange(grads.reshape(peers, rows // peers, width), plane)
    share = jnp.sum(parts.astype(F32), axis=0).astype(BF16)
    shares = exchange(jnp.broadcast_to(share[None], (depth,) + share.shape), "rep")
    share = jnp.sum(shares.astype(F32), axis=0).astype(BF16)
    parts = exchange(jnp.broadcast_to(share[None], (peers,) + share.shape), plane)
    return parts.reshape(rows, width).astype(F32)


def body(
    self_feat,
    neighbor,
    grad_out,
    fetch_rows,
    fetch_count,
    table_codes,
    table_scale,
    hot_table,
    self_weight,
    neighbor_weight,
):
    width = self_feat.shape[1]
    wanted = exchange(fetch_rows, "own")
    picks, table = prepare(neighbor, table_codes, table_scale)
    summed, words, held, grad_out = count_rows(
        picks, hot_table, self_feat, grad_out, self_weight, neighbor_weight
    )
    rows = exchange(select_rows(wanted, table), "own")
    hidden, grads = layer(fetch_count, summed, words, rows, held, grad_out)
    total = sum_everywhere(grads)
    return hidden, total[:width], total[width:]


def solution(mesh):
    split = P(("grp", "own", "rep"), None)
    in_specs = (
        split,
        split,
        split,
        split,
        P(("grp", "own", "rep")),
        P("own", None),
        P("own", None),
        P(),
        P(),
        P(),
    )
    out_specs = (split, P(), P())
    return jax.shard_map(body, mesh=mesh, in_specs=in_specs, out_specs=out_specs, check_vma=False)
```
